256 devices in a mesh: row: 16 (over y, x_hi, core), col: 16 (over x_lo, z).
Axes of the slice: x: 4 (x_hi: 2, x_lo: 2; x = x_hi * 2 + x_lo), y: 4, z: 8, core: 2. Of those that a mesh axis runs over, the one named last changes fastest.
Arguments:
- features: bfloat16 [16, 4096, 256], P('col', 'row'), may hold values from -6 to 6
- tile_values: bfloat16 [16, 16, 160, 128, 128], P('row', 'col'), may hold values from 0 to 0.17675781
- tile_rows: int32 [16, 16, 160], P('row', 'col'), may hold values from 0 to 31
- tile_cols: int32 [16, 16, 160], P('row', 'col'), may hold values from 0 to 31
- tile_counts: int32 [16, 16], P('row', 'col'), may hold values from 40 to 160, as said below
- weight: bfloat16 [256, 256], replicated, may hold values from -0.375 to 0.375
- cotangent: bfloat16 [16, 4096, 256], P('row', 'col'), may hold values from -6 to 6
Outputs:
- activated: bfloat16 [16, 4096, 256], P('row', 'col')
- weight_grad: float32 [256, 256], replicated
- feature_grad: bfloat16 [16, 4096, 256], P('col', 'row')
The draws below stay inside these ranges and needn't reach their ends.
Inputs may be any that keep to these rules, and one draw needn't show every extreme that they name: `tile_counts`: in every draw some grid block has exactly 160 live slots.
All inputs are finite; a program needn't handle non-finite values.
Results may differ from the reference program's by a relative error of at most 0.04.
Values may be sent and summed in bfloat16 or wider, within the bound.
No kernel may reach another device: no remote copies, remote signals or barrier semaphores. Data moves between devices by JAX's collectives and lax.ppermute only.
A program may use at most 128 MiB of HBM per device.

```python
import jax
import jax.numpy as jnp
from jax import lax

F = 256
TILE = 128
NODE_DEV = 256
TILES_DEV = 160
NODES = 65536
N_ROW = 16
N_COL = 16


def draw_tile_counts(key, part):
    key = jax.random.fold_in(key, 5)
    first, second = jax.random.split(key)
    counts = jax.random.randint(first, (N_ROW * N_COL,), TILES_DEV // 4, TILES_DEV + 1)
    chosen = jax.random.randint(second, (), 0, N_ROW * N_COL)
    flattened = jnp.where(jnp.arange(N_ROW * N_COL) == chosen, TILES_DEV, counts)
    return flattened.reshape(N_ROW, N_COL).astype(jnp.int32)


def plant(array, rng, low, largest):
    index_at = [jax.random.randint(jax.random.fold_in(rng, axis), (), 0, length) for axis, length in enumerate(array.shape)]
    longest = array.shape.index(max(array.shape))
    neighbour = index_at[:longest] + [(index_at[longest] + 1) % array.shape[longest]] + index_at[longest + 1:]
    return array.at[tuple(index_at)].set(low).at[tuple(neighbour)].set(largest)


def level_of(stream_key, extent, cuts, low, high):
    factor_of, own = 1.0, jax.random.fold_in(stream_key, 6)
    for dim, shards_of in cuts:
        draws = jnp.exp(jax.random.uniform(jax.random.fold_in(own, dim), (shards_of,), jnp.float32, low / len(cuts), high / len(cuts)))
        factor_of = factor_of * jnp.repeat(draws, extent[dim] // shards_of).reshape([-1 if axis == dim else 1 for axis in range(len(extent))])
    return factor_of


def centred(key, shape, spread, bound, pieces=(), kind=jnp.bfloat16):
    array = jax.random.normal(key, shape, jnp.float32) * spread
    if len(pieces) > 0:
        array = level_of(key, shape, pieces, -0.22, 0.18) * array
    return jnp.clip(array, min=-bound, max=bound).astype(kind)


def setup_inputs(seed: int = 0) -> dict:
    streams_of = jax.random.split(jax.random.key(seed), 8)
    return {
        "features": centred(streams_of[0], (N_COL, N_ROW * NODE_DEV, F), 1.0, 6.0, ((0, 16), (1, 16))),
        "tile_values": jnp.clip(0.17675781 * jax.random.uniform(streams_of[1], (N_ROW, N_COL, TILES_DEV, TILE, TILE), jnp.float32) ** level_of(streams_of[1], (N_ROW, N_COL, TILES_DEV, TILE, TILE), ((0, 16), (1, 16)), -0.2, 0.2), 0.0, 0.17675781).astype(jnp.bfloat16),
        "tile_rows": plant(jax.random.randint(streams_of[2], (N_ROW, N_COL, TILES_DEV), 0, N_COL * NODE_DEV // TILE), jax.random.fold_in(streams_of[2], 1), 0, (N_COL * NODE_DEV // TILE) - 1).astype(jnp.int32),
        "tile_cols": plant(jax.random.randint(streams_of[3], (N_ROW, N_COL, TILES_DEV), 0, N_ROW * NODE_DEV // TILE), jax.random.fold_in(streams_of[3], 1), 0, (N_ROW * NODE_DEV // TILE) - 1).astype(jnp.int32),
        "tile_counts": draw_tile_counts(jax.random.fold_in(streams_of[7], 71), 0),
        "weight": centred(streams_of[5], (F, F), F ** -0.5, 0.375),
        "cotangent": centred(streams_of[6], (N_ROW, N_COL * NODE_DEV, F), 1.0, 6.0, ((0, 16), (1, 16))),
    }


def value_masked_entries(tile_values, tile_counts, block_row, block_col):
    values = tile_values[block_row, block_col].astype(jnp.float32)
    slots = jnp.arange(TILES_DEV, dtype=jnp.int32)
    return jnp.where((slots < tile_counts[block_row, block_col])[:, None, None], values, jnp.zeros((), jnp.float32))


def reference(features, tile_values, tile_rows, tile_cols, tile_counts, weight, cotangent):
    row_span = N_COL * NODE_DEV
    column_extent = N_ROW * NODE_DEV
    flat_features = features.reshape(NODES, F)

    def forward_step(total, index):
        block_row = index // N_COL
        block_col = index % N_COL
        values = value_masked_entries(tile_values, tile_counts, block_row, block_col)
        sender_nodes = lax.dynamic_slice_in_dim(flat_features, (block_col * column_extent).astype(jnp.int32), column_extent, 0).astype(jnp.float32)
        picked = sender_nodes.reshape(column_extent // TILE, TILE, F)[tile_cols[block_row, block_col]]
        products = jnp.einsum("tab,tbf->taf", values, picked)
        summed = jnp.zeros((row_span // TILE, TILE, F), jnp.float32).at[tile_rows[block_row, block_col]].add(products)
        rounded = summed.reshape(row_span, F).astype(jnp.bfloat16).astype(jnp.float32)
        start = (block_row * row_span).astype(jnp.int32)
        current = lax.dynamic_slice_in_dim(total, start, row_span, 0)
        total = lax.dynamic_update_slice_in_dim(total, current + rounded, start, 0)
        return total, None

    block_ids = jnp.arange(N_ROW * N_COL, dtype=jnp.int32)
    summed_rows, _ = lax.scan(forward_step, jnp.zeros((NODES, F), jnp.float32), block_ids)
    aggregated = summed_rows.astype(jnp.bfloat16)
    pre = jnp.dot(aggregated, weight, preferred_element_type=jnp.float32)
    sigmoid_pre = jax.nn.sigmoid(pre)
    activated = (pre * sigmoid_pre).astype(jnp.bfloat16)
    slope = sigmoid_pre * (1.0 + pre * (1.0 - sigmoid_pre))
    upstream = (cotangent.reshape(NODES, F).astype(jnp.float32) * slope).astype(jnp.bfloat16)
    weight_grad = jnp.dot(aggregated.T, upstream, preferred_element_type=jnp.float32) * (NODES ** -0.5)
    down = jnp.dot(upstream, weight.T, preferred_element_type=jnp.float32).astype(jnp.bfloat16)

    def backward_step(total, index):
        block_row = index // N_COL
        block_col = index % N_COL
        values = value_masked_entries(tile_values, tile_counts, block_row, block_col)
        sender_nodes = lax.dynamic_slice_in_dim(down, (block_row * row_span).astype(jnp.int32), row_span, 0).astype(jnp.float32)
        picked = sender_nodes.reshape(row_span // TILE, TILE, F)[tile_rows[block_row, block_col]]
        products = jnp.einsum("tab,taf->tbf", values, picked)
        summed = jnp.zeros((column_extent // TILE, TILE, F), jnp.float32).at[tile_cols[block_row, block_col]].add(products)
        rounded = summed.reshape(column_extent, F).astype(jnp.bfloat16).astype(jnp.float32)
        start = (block_col * column_extent).astype(jnp.int32)
        current = lax.dynamic_slice_in_dim(total, start, column_extent, 0)
        total = lax.dynamic_update_slice_in_dim(total, current + rounded, start, 0)
        return total, None

    back_rows, _ = lax.scan(backward_step, jnp.zeros((NODES, F), jnp.float32), block_ids)
    feature_grad = back_rows.astype(jnp.bfloat16)
    return (activated.reshape(N_ROW, N_COL * NODE_DEV, F), weight_grad, feature_grad.reshape(N_COL, N_ROW * NODE_DEV, F))
```

```python
import functools

import jax
import jax.numpy as jnp
from jax import lax
from jax.experimental import pallas as pl
from jax.experimental.pallas import tpu as pltpu
from jax.sharding import PartitionSpec as P

GROUP = 16
VMEM = pl.BlockSpec(memory_space=pltpu.VMEM)
SMEM = pl.BlockSpec(memory_space=pltpu.SMEM)


def params(mib):
    return pltpu.CompilerParams(vmem_limit_bytes=mib * 2**20)


def spmm_kernel(transposed, pieces, live, dst, src, *refs):
    sources, (tiles, *outs, held, total) = refs[:pieces], refs[pieces:]
    tile = tiles.shape[-1]
    at = 0
    for piece in sources:
        held[at : at + piece.shape[0], :] = piece[...]
        at += piece.shape[0]
    total[...] = jnp.zeros_like(total)
    count = live[0]
    contract = (((0 if transposed else 1,), (0,)), ((), ()))

    def step(group, carry):
        products = []
        for unit in range(GROUP):
            slot = group * GROUP + unit
            rows = pl.ds(pl.multiple_of(src[slot] * tile, tile), tile)
            values = tiles[slot]
            values = jnp.where(slot < count, values, jnp.zeros_like(values))
            products.append(
                lax.dot_general(values, held[rows, :], contract, preferred_element_type=jnp.float32)
            )
        for unit in range(GROUP):
            rows = pl.ds(pl.multiple_of(dst[group * GROUP + unit] * tile, tile), tile)
            total[rows, :] += products[unit]
        return carry

    lax.fori_loop(0, (count + GROUP - 1) // GROUP, step, 0)
    at = 0
    for out in outs:
        out[...] = total[at : at + out.shape[0], :].astype(out.dtype)
        at += out.shape[0]


def spmm(transposed, live, dst, src, sources, tiles, parts):
    slots, tile, _ = tiles.shape
    width = sources[0].shape[1]
    depth = sum(piece.shape[0] for piece in sources)
    flops = 2 * slots * tile * tile * width
    out = pl.pallas_call(
        functools.partial(spmm_kernel, transposed, len(sources)),
        out_shape=[jax.ShapeDtypeStruct((depth // parts, width), jnp.bfloat16)] * parts,
        in_specs=[SMEM] * 3 + [VMEM] * (len(sources) + 1),
        out_specs=[VMEM] * parts,
        scratch_shapes=[
            pltpu.VMEM((depth, width), jnp.bfloat16),
            pltpu.VMEM((depth, width), jnp.float32),
        ],
        compiler_params=params(40),
        cost_estimate=pl.CostEstimate(
            flops=flops, bytes_accessed=9 * 2**20, transcendentals=0
        ),
        name="spmm_back" if transposed else "spmm",
    )(live, dst, src, *sources, tiles)
    return out


def dense_kernel(received, weight, cotangent, activated, down, weight_terms):
    sums = received[0].astype(jnp.float32)
    for part in range(1, received.shape[0]):
        sums += received[part].astype(jnp.float32)
    aggregated = sums.astype(jnp.bfloat16)
    pre = jnp.dot(aggregated, weight[...], preferred_element_type=jnp.float32)
    gate = jax.nn.sigmoid(pre)
    activated[...] = (pre * gate).astype(jnp.bfloat16)
    slope = gate * (1.0 + pre * (1.0 - gate))
    upstream = (cotangent[...].astype(jnp.float32) * slope).astype(jnp.bfloat16)
    down[...] = lax.dot_general(
        upstream, weight[...], (((1,), (1,)), ((), ())), preferred_element_type=jnp.float32
    ).astype(jnp.bfloat16)
    weight_terms[...] = lax.dot_general(
        aggregated, upstream, (((0,), (0,)), ((), ())), preferred_element_type=jnp.float32
    )


def dense(received, weight, cotangent):
    rows, width = cotangent.shape
    return pl.pallas_call(
        dense_kernel,
        out_shape=[
            jax.ShapeDtypeStruct((rows, width), jnp.bfloat16),
            jax.ShapeDtypeStruct((rows, width), jnp.bfloat16),
            jax.ShapeDtypeStruct((width, width), jnp.float32),
        ],
        in_specs=[VMEM] * 3,
        out_specs=[VMEM] * 3,
        compiler_params=params(24),
        name="dense",
    )(received, weight, cotangent)


def body(features, tile_values, tile_rows, tile_cols, tile_counts, weight, cotangent):
    node_rows, width = features.shape[1:]
    slots, tile = tile_values.shape[2:4]
    rows_n, cols_n = lax.axis_size("row"), lax.axis_size("col")
    chips = rows_n // 2
    core = lax.axis_index("row") % 2
    same_core = [[2 * k + c for k in range(chips)] for c in range(2)]
    swap = [(i, i ^ 1) for i in range(rows_n)]
    live = tile_counts.reshape(1)
    tiles = tile_values.reshape(slots, tile, tile)
    row_tiles = tile_rows.reshape(slots)
    per = node_rows // tile
    owner, inner = tile_cols.reshape(slots) // per, tile_cols.reshape(slots) % per
    col_tiles = ((((owner % 2) ^ core) * chips) + owner // 2) * per + inner

    own = lax.all_to_all(
        jnp.broadcast_to(features, (chips, node_rows, width)), "row", 0, 0,
        axis_index_groups=same_core, tiled=True,
    ).reshape(chips * node_rows, width)
    other = lax.ppermute(own, "row", swap)
    (block,) = spmm(False, live, row_tiles, col_tiles, [own, other], tiles, 1)
    received = lax.all_to_all(block.reshape(cols_n, node_rows, width), "col", 0, 0, tiled=True)
    activated, down, terms = dense(received, weight, cotangent.reshape(node_rows, width))

    down_all = lax.all_to_all(
        jnp.broadcast_to(down[None], (cols_n, node_rows, width)), "col", 0, 0, tiled=True
    ).reshape(cols_n * node_rows, width)

    share = lax.all_to_all(terms.reshape(rows_n, -1, width), "row", 0, 0, tiled=True)
    share = jnp.sum(share, axis=0)
    share = lax.all_to_all(share.reshape(cols_n, -1, width), "col", 0, 0, tiled=True)
    share = jnp.sum(share, axis=0) * float(node_rows * rows_n * cols_n) ** (-0.5)
    share = lax.all_to_all(
        jnp.broadcast_to(share[None], (cols_n, *share.shape)), "col", 0, 0, tiled=True
    ).reshape(-1, width)
    weight_grad = lax.all_to_all(
        jnp.broadcast_to(share[None], (rows_n, *share.shape)), "row", 0, 0, tiled=True
    ).reshape(width, width)

    mine, theirs = spmm(True, live, col_tiles, row_tiles, [down_all], tiles, 2)
    swapped = lax.ppermute(theirs, "row", swap)
    pair = (mine.astype(jnp.float32) + swapped.astype(jnp.float32)).astype(jnp.bfloat16)
    back = lax.all_to_all(
        pair.reshape(chips, node_rows, width), "row", 0, 0,
        axis_index_groups=same_core, tiled=True,
    )
    feature_grad = jnp.sum(back.astype(jnp.float32), axis=0).astype(jnp.bfloat16)
    return (
        activated.reshape(1, node_rows, width),
        weight_grad,
        feature_grad.reshape(1, node_rows, width),
    )


def solution(mesh):
    in_specs = (
        P("col", "row", None),
        P("row", "col", None, None, None),
        P("row", "col", None),
        P("row", "col", None),
        P("row", "col"),
        P(),
        P("row", "col", None),
    )
    out_specs = (P("row", "col", None), P(), P("col", "row", None))
    return jax.shard_map(body, mesh=mesh, in_specs=in_specs, out_specs=out_specs, check_vma=False)
```

```python
import functools

import jax
import jax.numpy as jnp
from jax import lax
from jax.experimental import pallas as pl
from jax.experimental.pallas import tpu as pltpu
from jax.sharding import PartitionSpec as P

GROUP = 32
VMEM = pl.BlockSpec(memory_space=pltpu.VMEM)
SMEM = pl.BlockSpec(memory_space=pltpu.SMEM)
HBM = pl.BlockSpec(memory_space=pltpu.HBM)
DMA = pltpu.SemaphoreType.DMA


def params(mib):
    return pltpu.CompilerParams(vmem_limit_bytes=mib * 2**20)


def shape(dtype, *dims):
    return jax.ShapeDtypeStruct(dims, dtype)


def f32(ref):
    return ref[...].astype(jnp.float32)


def copy_all(pairs, sems):
    copies = [pltpu.make_async_copy(a, b, sems.at[i]) for i, (a, b) in enumerate(pairs)]
    for copy in copies:
        copy.start()
    for copy in copies:
        copy.wait()


def spread_kernel(source, out, sems):
    copy_all([(source, out.at[i]) for i in range(out.shape[0])], sems)


def spread(source, copies):
    return pl.pallas_call(
        spread_kernel,
        out_shape=shape(source.dtype, copies, *source.shape),
        in_specs=[VMEM],
        out_specs=HBM,
        scratch_shapes=[DMA((copies,))],
        compiler_params=params(4),
        name="spread",
    )(source)


def spmm_kernel(transposed, pieces, live, dst, src, *refs):
    sources, tiles = refs[: len(pieces)], refs[len(pieces)]
    outs = refs[len(pieces) + 1 : -4]
    held, total, buffer, sems = refs[-4:]
    tile = tiles.shape[-1]
    count = live[0]
    groups = (count + GROUP - 1) // GROUP

    def load(group):
        slots = pl.ds(group * GROUP, GROUP)
        return pltpu.make_async_copy(tiles.at[slots], buffer.at[slots], sems.at[group])

    def begin(group, carry):
        load(group).start()
        return carry

    lax.fori_loop(0, groups, begin, 0)
    at = 0
    for rows, piece in zip(pieces, sources):
        held[at : at + rows, :] = piece[:rows, :]
        at += rows
    total[...] = jnp.zeros_like(total)
    contract = (((0 if transposed else 1,), (0,)), ((), ()))

    def step(group, carry):
        load(group).wait()
        products = []
        for unit in range(GROUP):
            slot = group * GROUP + unit
            rows = pl.ds(pl.multiple_of(src[slot] * tile, tile), tile)
            values = buffer[slot]
            values = jnp.where(slot < count, values, jnp.zeros_like(values))
            products.append(
                lax.dot_general(values, held[rows, :], contract, preferred_element_type=jnp.float32)
            )
        for unit in range(GROUP):
            rows = pl.ds(pl.multiple_of(dst[group * GROUP + unit] * tile, tile), tile)
            total[rows, :] += products[unit]
        return carry

    lax.fori_loop(0, groups, step, 0)
    at = 0
    for out in outs:
        out[...] = total[at : at + out.shape[0], :].astype(out.dtype)
        at += out.shape[0]


def spmm(transposed, live, dst, src, sources, pieces, tiles, parts):
    slots, tile, _ = tiles.shape
    width = sources[0].shape[1]
    depth = sum(pieces)
    return pl.pallas_call(
        functools.partial(spmm_kernel, transposed, pieces),
        out_shape=[shape(jnp.bfloat16, rows, width) for rows in parts],
        in_specs=[SMEM] * 3 + [VMEM] * len(sources) + [HBM],
        out_specs=[VMEM] * len(parts),
        scratch_shapes=[
            pltpu.VMEM((depth, width), jnp.bfloat16),
            pltpu.VMEM((depth, width), jnp.float32),
            pltpu.VMEM(tiles.shape, tiles.dtype),
            DMA((slots // GROUP,)),
        ],
        compiler_params=params(20),
        cost_estimate=pl.CostEstimate(
            flops=20 * slots * tile * tile * width, bytes_accessed=36 * 2**20, transcendentals=0
        ),
        name="spmm_back" if transposed else "spmm",
    )(live, dst, src, *sources, pltpu.with_memory_space_constraint(tiles, pltpu.HBM))


def add_at_kernel(start, first, second, out):
    end = start + second.shape[0]
    out[start:end, :] = (first[start:end, :].astype(jnp.float32) + f32(second)).astype(out.dtype)
    if start > 0:
        out[:start, :] = first[:start, :]
    if end < out.shape[0]:
        out[end:, :] = first[end:, :]


def add_at(first, second, start=0):
    return pl.pallas_call(
        functools.partial(add_at_kernel, start),
        out_shape=shape(first.dtype, *first.shape),
        in_specs=[VMEM] * 2,
        out_specs=VMEM,
        compiler_params=params(6),
        name="add_at",
    )(first, second)


def part_sum(parts):
    sums = parts[0].astype(jnp.float32)
    for part in range(1, parts.shape[0]):
        sums += parts[part].astype(jnp.float32)
    return sums


def split_sum_kernel(own, first, second, mine, theirs):
    sums = f32(own) + f32(first) + f32(second)
    mine[...] = sums[: mine.shape[0]]
    theirs[...] = sums[mine.shape[0] :].astype(theirs.dtype)


def split_sum(own, first, second):
    rows, width = own.shape
    return pl.pallas_call(
        split_sum_kernel,
        out_shape=[shape(jnp.float32, rows // 2, width), shape(own.dtype, rows // 2, width)],
        in_specs=[VMEM] * 3,
        out_specs=[VMEM] * 2,
        compiler_params=params(4),
        name="split_sum",
    )(own, first, second)


def whole_sum_kernel(parts, out):
    out[...] = part_sum(parts).astype(out.dtype)


def whole_sum(parts):
    return pl.pallas_call(
        whole_sum_kernel,
        out_shape=shape(parts.dtype, *parts.shape[1:]),
        in_specs=[VMEM],
        out_specs=VMEM,
        compiler_params=params(6),
        name="whole_sum",
    )(parts)


def dense_kernel(mine, swapped, weight, cotangent, activated, sent):
    rows = cotangent.shape[0]
    aggregated = (mine[...] + f32(swapped)).astype(jnp.bfloat16)
    pre = jnp.dot(aggregated, weight[...], preferred_element_type=jnp.float32)
    gate = jax.nn.sigmoid(pre)
    slope = gate * (1.0 + pre * (1.0 - gate))
    upstream = (cotangent[...].astype(jnp.float32) * slope).astype(jnp.bfloat16)
    sent[:rows, :] = lax.dot_general(
        upstream, weight[...], (((1,), (1,)), ((), ())), preferred_element_type=jnp.float32
    ).astype(jnp.bfloat16)
    sent[rows:, :] = lax.dot_general(
        aggregated, upstream, (((0,), (0,)), ((), ())), preferred_element_type=jnp.float32
    ).astype(jnp.bfloat16)
    activated[...] = (pre * gate).astype(jnp.bfloat16)


def dense(mine, swapped, weight, cotangent):
    rows, width = cotangent.shape
    return pl.pallas_call(
        dense_kernel,
        out_shape=[
            shape(jnp.bfloat16, rows, width),
            shape(jnp.bfloat16, rows + width, width),
        ],
        in_specs=[VMEM] * 4,
        out_specs=[VMEM] * 2,
        compiler_params=params(12),
        name="dense",
    )(mine, swapped, weight, cotangent)


def begin_kernel(place, sent, received, pair, rising, sums):
    rows = pair.shape[0] // 2
    along, part = sums.shape[:2]
    for out in (pair, rising):
        out[:rows, :] = sent[:rows, :]
        out[rows : 2 * rows, :] = received[:rows, :]
    for i in range(along):
        at = slice(rows + i * part, rows + (i + 1) * part)
        sums[i] = sent[at, :].astype(jnp.float32) + received[at, :].astype(jnp.float32)
    far = lax.rem(place[0] + along // 2, along)
    rising[2 * rows :, :] = sums[far].astype(rising.dtype)


def begin(place, sent, received, rows, along):
    width = sent.shape[1]
    part = (sent.shape[0] - rows) // along
    return pl.pallas_call(
        begin_kernel,
        out_shape=[
            shape(sent.dtype, 2 * rows, width),
            shape(sent.dtype, 2 * rows + part, width),
            shape(jnp.float32, along, part, width),
        ],
        in_specs=[SMEM] + [VMEM] * 2,
        out_specs=[VMEM] * 3,
        compiler_params=params(8),
        name="begin",
    )(place, sent, received)


def pass_on_kernel(first, last, offset, held, place, arrived, sums, out):
    rows = last - first
    along, part = sums.shape[:2]
    out[:rows, :] = arrived[first:last, :]
    term = sums[lax.rem(place[0] + offset, along)]
    if arrived.shape[0] > held:
        term += arrived[held:, :].astype(jnp.float32)
    out[rows:, :] = term.astype(out.dtype)


def pass_on(first, last, offset, held, place, arrived, sums):
    _, part, width = sums.shape
    return pl.pallas_call(
        functools.partial(pass_on_kernel, first, last, offset, held),
        out_shape=shape(arrived.dtype, last - first + part, width),
        in_specs=[SMEM] + [VMEM] * 2,
        out_specs=VMEM,
        compiler_params=params(6),
        name="pass_on",
    )(place, arrived, sums)


def ring_sum_kernel(place, rising, falling, sums, out, stage, sems):
    part = sums.shape[1]
    total = sums[place[0]]
    total += rising[rising.shape[0] - part :, :].astype(jnp.float32)
    total += falling[falling.shape[0] - part :, :].astype(jnp.float32)
    stage[...] = total.astype(stage.dtype)
    copy_all([(stage, out.at[i]) for i in range(out.shape[0])], sems)


def ring_sum(place, rising, falling, sums, copies):
    _, part, width = sums.shape
    return pl.pallas_call(
        ring_sum_kernel,
        out_shape=shape(rising.dtype, copies, part, width),
        in_specs=[SMEM] + [VMEM] * 3,
        out_specs=HBM,
        scratch_shapes=[pltpu.VMEM((part, width), rising.dtype), DMA((copies,))],
        compiler_params=params(4),
        name="ring_sum",
    )(place, rising, falling, sums)


def scaled_sum_kernel(scale, parts, out):
    out[...] = part_sum(parts) * scale


def scaled_sum(parts, scale):
    return pl.pallas_call(
        functools.partial(scaled_sum_kernel, scale),
        out_shape=shape(jnp.float32, *parts.shape[1:]),
        in_specs=[VMEM],
        out_specs=VMEM,
        compiler_params=params(4),
        name="scaled_sum",
    )(parts)


def arrange_kernel(place, *refs):
    pieces, out = refs[:-1], refs[-1]
    part = pieces[0].shape[0]
    for turn, piece in enumerate(pieces):
        at = lax.rem(place[0] + turn, len(pieces))
        out[pl.ds(pl.multiple_of(at * part, part), part), :] = piece[...]


def arrange(place, pieces):
    part, width = pieces[0].shape
    return pl.pallas_call(
        arrange_kernel,
        out_shape=shape(pieces[0].dtype, part * len(pieces), width),
        in_specs=[SMEM] + [VMEM] * len(pieces),
        out_specs=VMEM,
        compiler_params=params(4),
        name="arrange",
    )(place, *pieces)


def body(features, tile_values, tile_rows, tile_cols, tile_counts, weight, cotangent):
    node_rows, width = features.shape[1:]
    slots, tile = tile_values.shape[2:4]
    rows_n, cols_n = lax.axis_size("row"), lax.axis_size("col")
    chips, along = rows_n // 2, cols_n // 2
    core, side = lax.axis_index("row") % 2, lax.axis_index("col") // along
    place = lax.axis_index("col") % along
    same_core = [[2 * k + c for k in range(chips)] for c in range(2)]
    core_swap = [(i, i ^ 1) for i in range(rows_n)]
    side_swap = [(i, (i + along) % cols_n) for i in range(cols_n)]
    up = [(i, i - i % along + (i + 1) % along) for i in range(cols_n)]
    back = [(j, i) for i, j in up]
    live = tile_counts.reshape(1)
    tiles = tile_values.reshape(slots, tile, tile)
    per = node_rows // tile

    col_owner, col_inner = tile_cols.reshape(slots) // per, tile_cols.reshape(slots) % per
    by_core = ((((col_owner % 2) ^ core) * chips) + col_owner // 2) * per + col_inner
    row_owner, row_inner = tile_rows.reshape(slots) // per, tile_rows.reshape(slots) % per
    far = along // 2
    distance = (row_owner % along - place + along) % along
    nearest = jnp.where(
        distance < far, 2 * distance, jnp.where(distance == far, along - 1, 2 * (along - distance) - 1)
    )
    farthest = jnp.where(
        distance == 0, along - 1,
        jnp.where(distance <= far, along - 1 - 2 * distance + (distance == far), 2 * distance - along),
    )
    within = ((row_owner // along) ^ side) * per + row_inner
    by_nearest, by_farthest = nearest * 2 * per + within, farthest * 2 * per + within

    def exchange(x, axis, groups=None):
        return lax.all_to_all(x, axis, 0, 0, axis_index_groups=groups, tiled=True)

    def flat(x):
        return x.reshape(-1, x.shape[-1])

    own = flat(exchange(spread(features.reshape(node_rows, width), chips), "row", same_core))
    other = lax.ppermute(own, "row", core_swap)
    pair = 2 * node_rows
    blocks = spmm(
        False, live, by_farthest, by_core, [own, other], [chips * node_rows] * 2, tiles,
        [node_rows] * 2 + [pair] * (along - 1),
    )
    rising, falling = blocks[0], blocks[1]
    for step in range(1, far):
        rising = lax.ppermute(rising, "col", up)
        falling = lax.ppermute(falling, "col", back)
        rising = add_at(blocks[2 * step], rising)
        falling = add_at(blocks[2 * step + 1], falling, pair - falling.shape[0])
    rising = lax.ppermute(rising, "col", up)
    falling = lax.ppermute(falling, "col", back)
    mine, theirs = split_sum(blocks[-1], rising, falling)
    swapped = lax.ppermute(theirs, "col", side_swap)
    spot = place.reshape(1)
    activated, sent = dense(mine, swapped, weight, cotangent.reshape(node_rows, width))

    received = lax.ppermute(sent, "col", side_swap)
    both, rising, sums = begin(spot, sent, received, node_rows, along)
    falling = both
    sources = [both]
    for step in range(1, far):
        rising = lax.ppermute(rising, "col", up)
        falling = lax.ppermute(falling, "col", back)
        sources += [rising, falling]
        cut = node_rows if step == far - 1 else 0
        rising = pass_on(0, pair - cut, far - step, pair, spot, rising, sums)
        falling = pass_on(cut, pair, far + step, pair, spot, falling, sums)
    rising = lax.ppermute(rising, "col", up)
    falling = lax.ppermute(falling, "col", back)
    sources += [rising, falling]
    terms = ring_sum(spot, rising, falling, sums, rows_n)
    terms, *sources = lax.optimization_barrier((terms, *sources))
    terms = exchange(terms, "row")

    mine, theirs = spmm(
        True, live, by_core, by_nearest, sources, [pair] * (along - 1) + [node_rows] * 2,
        tiles, [chips * node_rows] * 2,
    )
    scale = float(node_rows * rows_n * cols_n) ** (-0.5)
    own_share = scaled_sum(terms, scale)
    own_share, mine, theirs = lax.optimization_barrier((own_share, mine, theirs))
    shares = add_at(mine, lax.ppermute(theirs, "row", core_swap))
    shares = exchange(shares.reshape(chips, node_rows, width), "row", same_core)
    feature_grad = whole_sum(shares)

    turned = [
        lax.ppermute(
            own_share, "col", [(i, i - i % along + (i - turn) % along) for i in range(cols_n)]
        )
        for turn in range(1, along)
    ]
    weight_grad = arrange(spot, [own_share] + turned)
    return (
        activated.reshape(1, node_rows, width),
        weight_grad,
        feature_grad.reshape(1, node_rows, width),
    )


def solution(mesh):
    in_specs = (
        P("col", "row", None),
        P("row", "col", None, None, None),
        P("row", "col", None),
        P("row", "col", None),
        P("row", "col"),
        P(),
        P("row", "col", None),
    )
    out_specs = (P("row", "col", None), P(), P("col", "row", None))
    return jax.shard_map(body, mesh=mesh, in_specs=in_specs, out_specs=out_specs, check_vma=False)
```

```python
import functools

import jax
import jax.numpy as jnp
from jax import lax
from jax.experimental import pallas as pl
from jax.experimental.pallas import tpu as pltpu
from jax.sharding import PartitionSpec as P

GROUP = 32
VMEM = pl.BlockSpec(memory_space=pltpu.VMEM)
SMEM = pl.BlockSpec(memory_space=pltpu.SMEM)
HBM = pl.BlockSpec(memory_space=pltpu.HBM)
DMA = pltpu.SemaphoreType.DMA


def params(mib):
    return pltpu.CompilerParams(vmem_limit_bytes=mib * 2**20)


def shape(dtype, *dims):
    return jax.ShapeDtypeStruct(dims, dtype)


def f32(ref):
    return ref[...].astype(jnp.float32)


def copy_all(pairs, sems):
    copies = [pltpu.make_async_copy(a, b, sems.at[i]) for i, (a, b) in enumerate(pairs)]
    for copy in copies:
        copy.start()
    for copy in copies:
        copy.wait()


def spmm_kernel(transposed, pieces, live, dst, src, *refs):
    sources, tiles = refs[: len(pieces)], refs[len(pieces)]
    outs = refs[len(pieces) + 1 : -4]
    held, total, buffer, sems = refs[-4:]
    tile = tiles.shape[-1]
    count = live[0]
    groups = (count + GROUP - 1) // GROUP

    def load(group):
        slots = pl.ds(group * GROUP, GROUP)
        return pltpu.make_async_copy(tiles.at[slots], buffer.at[slots], sems.at[group])

    def begin(group, carry):
        load(group).start()
        return carry

    lax.fori_loop(0, groups, begin, 0)
    at = 0
    for rows, piece in zip(pieces, sources):
        held[at : at + rows, :] = piece[:rows, :]
        at += rows
    total[...] = jnp.zeros_like(total)
    contract = (((0 if transposed else 1,), (0,)), ((), ()))

    def step(group, carry):
        load(group).wait()
        products = []
        for unit in range(GROUP):
            slot = group * GROUP + unit
            rows = pl.ds(pl.multiple_of(src[slot] * tile, tile), tile)
            values = buffer[slot]
            values = jnp.where(slot < count, values, jnp.zeros_like(values))
            products.append(
                lax.dot_general(values, held[rows, :], contract, preferred_element_type=jnp.float32)
            )
        for unit in range(GROUP):
            rows = pl.ds(pl.multiple_of(dst[group * GROUP + unit] * tile, tile), tile)
            total[rows, :] += products[unit]
        return carry

    lax.fori_loop(0, groups, step, 0)
    at = 0
    for out in outs:
        out[...] = total[at : at + out.shape[0], :].astype(out.dtype)
        at += out.shape[0]


def spmm(transposed, live, dst, src, sources, pieces, tiles, parts):
    slots, tile, _ = tiles.shape
    width = sources[0].shape[1]
    depth = sum(pieces)
    return pl.pallas_call(
        functools.partial(spmm_kernel, transposed, pieces),
        out_shape=[shape(jnp.bfloat16, rows, width) for rows in parts],
        in_specs=[SMEM] * 3 + [VMEM] * len(sources) + [HBM],
        out_specs=[VMEM] * len(parts),
        scratch_shapes=[
            pltpu.VMEM((depth, width), jnp.bfloat16),
            pltpu.VMEM((depth, width), jnp.float32),
            pltpu.VMEM(tiles.shape, tiles.dtype),
            DMA((slots // GROUP,)),
        ],
        compiler_params=params(20),
        cost_estimate=pl.CostEstimate(
            flops=20 * slots * tile * tile * width, bytes_accessed=36 * 2**20, transcendentals=0
        ),
        name="spmm_back" if transposed else "spmm",
    )(live, dst, src, *sources, pltpu.with_memory_space_constraint(tiles, pltpu.HBM))


def add_kernel(first, second, out):
    out[...] = (f32(first) + f32(second)).astype(out.dtype)


def add(first, second):
    return pl.pallas_call(
        add_kernel,
        out_shape=shape(first.dtype, *first.shape),
        in_specs=[VMEM] * 2,
        out_specs=VMEM,
        compiler_params=params(6),
        name="add",
    )(first, second)


def ring_add_kernel(upper, rising, lower, falling, rising_out, falling_out):
    end = rising.shape[0]
    rising_out[:end, :] = (upper[:end, :].astype(jnp.float32) + f32(rising)).astype(upper.dtype)
    if end < upper.shape[0]:
        rising_out[end:, :] = upper[end:, :]
    start = lower.shape[0] - falling.shape[0]
    falling_out[start:, :] = (lower[start:, :].astype(jnp.float32) + f32(falling)).astype(
        lower.dtype
    )
    if start > 0:
        falling_out[:start, :] = lower[:start, :]


def ring_add(upper, rising, lower, falling):
    return pl.pallas_call(
        ring_add_kernel,
        out_shape=[shape(upper.dtype, *upper.shape)] * 2,
        in_specs=[VMEM] * 4,
        out_specs=[VMEM] * 2,
        compiler_params=params(8),
        name="ring_add",
    )(upper, rising, lower, falling)


def part_sum(parts):
    sums = parts[0].astype(jnp.float32)
    for part in range(1, parts.shape[0]):
        sums += parts[part].astype(jnp.float32)
    return sums


def fold_kernel(own, first, second, out):
    out[...] = (f32(own) + f32(first) + f32(second)).astype(out.dtype)


def fold(own, first, second):
    return pl.pallas_call(
        fold_kernel,
        out_shape=shape(own.dtype, *own.shape),
        in_specs=[VMEM] * 3,
        out_specs=VMEM,
        compiler_params=params(4),
        name="fold",
    )(own, first, second)


def whole_sum_kernel(parts, out):
    out[...] = part_sum(parts).astype(out.dtype)


def whole_sum(parts):
    return pl.pallas_call(
        whole_sum_kernel,
        out_shape=shape(parts.dtype, *parts.shape[1:]),
        in_specs=[VMEM],
        out_specs=VMEM,
        compiler_params=params(6),
        name="whole_sum",
    )(parts)


def dense_kernel(chain, last, place, own, other, weight, cotangent, other_cotangent, *refs):
    rows = own.shape[0] // 2
    at_rows = slice(chain * rows, (chain + 1) * rows)
    if last:
        before, pair_before, terms_before, activated, pair, rising, sums = refs
        activated[: chain * rows, :] = before[...]
    else:
        activated, pair, terms_out = refs
    terms = []
    for at, cot in ((0, cotangent), (rows, other_cotangent)):
        there = rows - at
        aggregated = (
            own[at : at + rows, :].astype(jnp.float32)
            + other[there : there + rows, :].astype(jnp.float32)
        ).astype(jnp.bfloat16)
        pre = jnp.dot(aggregated, weight[...], preferred_element_type=jnp.float32)
        gate = jax.nn.sigmoid(pre)
        slope = gate * (1.0 + pre * (1.0 - gate))
        upstream = (cot[at_rows, :].astype(jnp.float32) * slope).astype(jnp.bfloat16)
        down = lax.dot_general(
            upstream, weight[...], (((1,), (1,)), ((), ())), preferred_element_type=jnp.float32
        ).astype(jnp.bfloat16)
        if last:
            for out in (pair, rising):
                out[2 * at : 2 * at + rows, :] = pair_before[at : at + rows, :]
                out[2 * at + rows : 2 * at + 2 * rows, :] = down
        else:
            pair[at : at + rows, :] = down
        terms.append(
            lax.dot_general(
                aggregated, upstream, (((0,), (0,)), ((), ())), preferred_element_type=jnp.float32
            )
        )
        if at == 0:
            activated[at_rows if last else slice(None), :] = (pre * gate).astype(jnp.bfloat16)
    total = terms[0] + terms[1]
    if last:
        along = sums.shape[0]
        sums[...] = (terms_before[...] + total).reshape(sums.shape)
        far = lax.rem(place[0] + along // 2, along)
        rising[pair.shape[0] :, :] = sums[far].astype(rising.dtype)
    else:
        terms_out[...] = total


def dense(chain, place, own, other, weight, cotangent, other_cotangent, along, before=()):
    rows, width = own.shape[0] // 2, own.shape[1]
    part = width // along
    if before:
        out = [
            shape(jnp.bfloat16, 2 * rows, width),
            shape(jnp.bfloat16, 4 * rows, width),
            shape(jnp.bfloat16, 4 * rows + part, width),
            shape(jnp.float32, along, part, width),
        ]
    else:
        out = [
            shape(jnp.bfloat16, rows, width),
            shape(jnp.bfloat16, 2 * rows, width),
            shape(jnp.float32, width, width),
        ]
    return pl.pallas_call(
        functools.partial(dense_kernel, chain, bool(before)),
        out_shape=out,
        in_specs=[SMEM] + [VMEM] * (5 + len(before)),
        out_specs=[VMEM] * len(out),
        compiler_params=params(16),
        name="dense",
    )(place, own, other, weight, cotangent, other_cotangent, *before)


def pass_on_kernel(cut, offsets, held, place, rising, falling, sums, rising_out, falling_out):
    along, part = sums.shape[:2]
    for first, last, offset, arrived, out in (
        (0, held - cut, offsets[0], rising, rising_out),
        (cut, held, offsets[1], falling, falling_out),
    ):
        out[: last - first, :] = arrived[first:last, :]
        term = sums[lax.rem(place[0] + offset, along)]
        if arrived.shape[0] > held:
            term += arrived[held:, :].astype(jnp.float32)
        out[last - first :, :] = term.astype(out.dtype)


def pass_on(cut, offsets, held, place, rising, falling, sums):
    _, part, width = sums.shape
    return pl.pallas_call(
        functools.partial(pass_on_kernel, cut, offsets, held),
        out_shape=[shape(rising.dtype, held - cut + part, width)] * 2,
        in_specs=[SMEM] + [VMEM] * 3,
        out_specs=[VMEM] * 2,
        compiler_params=params(8),
        name="pass_on",
    )(place, rising, falling, sums)


def ring_sum_kernel(place, rising, falling, sums, out, stage, sems):
    part = sums.shape[1]
    total = sums[place[0]]
    total += rising[rising.shape[0] - part :, :].astype(jnp.float32)
    total += falling[falling.shape[0] - part :, :].astype(jnp.float32)
    stage[...] = total.astype(stage.dtype)
    copy_all([(stage, out.at[i]) for i in range(out.shape[0])], sems)


def ring_sum(place, rising, falling, sums, copies):
    _, part, width = sums.shape
    return pl.pallas_call(
        ring_sum_kernel,
        out_shape=shape(rising.dtype, copies, part, width),
        in_specs=[SMEM] + [VMEM] * 3,
        out_specs=HBM,
        scratch_shapes=[pltpu.VMEM((part, width), rising.dtype), DMA((copies,))],
        compiler_params=params(4),
        name="ring_sum",
    )(place, rising, falling, sums)


def scaled_sum_kernel(scale, parts, out):
    out[...] = part_sum(parts) * scale


def scaled_sum(parts, scale):
    return pl.pallas_call(
        functools.partial(scaled_sum_kernel, scale),
        out_shape=shape(jnp.float32, *parts.shape[1:]),
        in_specs=[VMEM],
        out_specs=VMEM,
        compiler_params=params(4),
        name="scaled_sum",
    )(parts)


def arrange_kernel(place, *refs):
    pieces, out = refs[:-1], refs[-1]
    part = pieces[0].shape[0]
    for turn, piece in enumerate(pieces):
        at = lax.rem(place[0] + turn, len(pieces))
        out[pl.ds(pl.multiple_of(at * part, part), part), :] = piece[...]


def arrange(place, pieces):
    part, width = pieces[0].shape
    return pl.pallas_call(
        arrange_kernel,
        out_shape=shape(pieces[0].dtype, part * len(pieces), width),
        in_specs=[SMEM] + [VMEM] * len(pieces),
        out_specs=VMEM,
        compiler_params=params(4),
        name="arrange",
    )(place, *pieces)


def body(features, tile_values, tile_rows, tile_cols, tile_counts, weight, cotangent):
    node_rows, width = features.shape[1:]
    slots, tile = tile_values.shape[2:4]
    rows_n, cols_n = lax.axis_size("row"), lax.axis_size("col")
    chips, along = rows_n // 2, cols_n // 2
    core, side = lax.axis_index("row") % 2, lax.axis_index("col") // along
    place = lax.axis_index("col") % along
    same_core = [[2 * k + c for k in range(chips)] for c in range(2)]
    core_swap = [(i, i ^ 1) for i in range(rows_n)]
    side_swap = [(i, (i + along) % cols_n) for i in range(cols_n)]
    up = [(i, i - i % along + (i + 1) % along) for i in range(cols_n)]
    back = [(j, i) for i, j in up]
    live = tile_counts.reshape(1)
    tiles = tile_values.reshape(slots, tile, tile)
    per = node_rows // tile

    col_owner, col_inner = tile_cols.reshape(slots) // per, tile_cols.reshape(slots) % per
    by_core = ((((col_owner % 2) ^ core) * chips) + col_owner // 2) * per + col_inner
    row_owner, row_inner = tile_rows.reshape(slots) // per, tile_rows.reshape(slots) % per
    far = along // 2
    distance = (row_owner % along - place + along) % along
    nearest = jnp.where(
        distance < far, 2 * distance, jnp.where(distance == far, along - 1, 2 * (along - distance) - 1)
    )
    farthest = jnp.where(
        distance == 0, along - 1,
        jnp.where(distance <= far, along - 1 - 2 * distance + (distance == far), 2 * distance - along),
    )
    row_side = (row_owner // along) ^ side
    by_nearest = (nearest * 2 + row_side) * per + row_inner
    by_farthest = (row_inner * along + farthest) * 2 + row_side

    def exchange(x, axis, groups=None):
        return lax.all_to_all(x, axis, 0, 0, axis_index_groups=groups, tiled=True)

    def flat(x):
        return x.reshape(-1, x.shape[-1])

    own = flat(
        exchange(jnp.broadcast_to(features, (chips, node_rows, width)), "row", same_core)
    )
    other = lax.ppermute(own, "row", core_swap)
    pair = 2 * tile
    sizes = [tile] * 2 + [pair] * (along - 1)
    blocks = spmm(
        False, live, by_farthest, by_core, [own, other], [chips * node_rows] * 2, tiles, sizes * per
    )
    chains = range(per)
    blocks = [blocks[c * len(sizes) : (c + 1) * len(sizes)] for c in chains]
    cotangent = cotangent.reshape(node_rows, width)
    other_cotangent = lax.ppermute(cotangent, "col", side_swap)
    rings = [(blocks[c][0], blocks[c][1]) for c in chains]

    def turn(ring):
        return lax.ppermute(ring[0], "col", up), lax.ppermute(ring[1], "col", back)

    for step in range(1, far):
        for c in chains:
            rising, falling = turn(rings[c])
            if step == 1 and c == 0:
                rising, falling, other_cotangent = lax.optimization_barrier(
                    (rising, falling, other_cotangent)
                )
            rings[c] = ring_add(blocks[c][2 * step], rising, blocks[c][2 * step + 1], falling)
    own_sums = [fold(blocks[c][-1], *turn(rings[c])) for c in chains]
    other_sums = [lax.ppermute(own_sums[c], "col", side_swap) for c in chains]
    spot = place.reshape(1)
    dense_args = (weight, cotangent, other_cotangent, along)
    first = dense(0, spot, own_sums[0], other_sums[0], *dense_args)
    activated, both, rising, sums = dense(
        1, spot, own_sums[1], other_sums[1], *dense_args, first
    )

    pair = 2 * node_rows
    falling = both
    sources = [both]
    for step in range(1, far):
        rising = lax.ppermute(rising, "col", up)
        falling = lax.ppermute(falling, "col", back)
        sources += [rising, falling]
        cut = node_rows if step == far - 1 else 0
        rising, falling = pass_on(
            cut, (far - step, far + step), pair, spot, rising, falling, sums
        )
    rising = lax.ppermute(rising, "col", up)
    falling = lax.ppermute(falling, "col", back)
    sources += [rising, falling]
    terms = ring_sum(spot, rising, falling, sums, chips)
    terms, *sources = lax.optimization_barrier((terms, *sources))
    terms = exchange(terms, "row", same_core)

    mine, theirs = spmm(
        True, live, by_core, by_nearest, sources, [pair] * (along - 1) + [node_rows] * 2,
        tiles, [chips * node_rows] * 2,
    )
    share = scaled_sum(terms, float(node_rows * rows_n * cols_n) ** (-0.5))
    share, mine, theirs = lax.optimization_barrier((share, mine, theirs))
    shares = add(mine, lax.ppermute(theirs, "row", core_swap))
    share = add(share, lax.ppermute(share, "row", core_swap))
    shares = exchange(shares.reshape(chips, node_rows, width), "row", same_core)
    feature_grad = whole_sum(shares)

    turned = [
        lax.ppermute(
            share, "col", [(i, i - i % along + (i - turn) % along) for i in range(cols_n)]
        )
        for turn in range(1, along)
    ]
    weight_grad = arrange(spot, [share] + turned)
    return (
        activated.reshape(1, node_rows, width),
        weight_grad,
        feature_grad.reshape(1, node_rows, width),
    )


def solution(mesh):
    in_specs = (
        P("col", "row", None),
        P("row", "col", None, None, None),
        P("row", "col", None),
        P("row", "col", None),
        P("row", "col"),
        P(),
        P("row", "col", None),
    )
    out_specs = (P("row", "col", None), P(), P("col", "row", None))
    return jax.shard_map(body, mesh=mesh, in_specs=in_specs, out_specs=out_specs, check_vma=False)
```

```python
import functools

import jax
import jax.numpy as jnp
from jax import lax
from jax.experimental import pallas as pl
from jax.experimental.pallas import tpu as pltpu
from jax.sharding import PartitionSpec as P

GROUP = 16
VMEM = pl.BlockSpec(memory_space=pltpu.VMEM)
SMEM = pl.BlockSpec(memory_space=pltpu.SMEM)
HBM = pl.BlockSpec(memory_space=pltpu.HBM)
DMA = pltpu.SemaphoreType.DMA


def params(mib):
    return pltpu.CompilerParams(vmem_limit_bytes=mib * 2**20)


def shape(dtype, *dims):
    return jax.ShapeDtypeStruct(dims, dtype)


def f32(ref):
    return ref[...].astype(jnp.float32)


def copy_all(pairs, sems):
    copies = [pltpu.make_async_copy(a, b, sems.at[i]) for i, (a, b) in enumerate(pairs)]
    for copy in copies:
        copy.start()
    for copy in copies:
        copy.wait()


def spmm_kernel(transposed, pieces, live, dst, src, *refs):
    sources, tiles = refs[: len(pieces)], refs[len(pieces)]
    outs = refs[len(pieces) + 1 : -4]
    held, total, buffer, sems = refs[-4:]
    tile = tiles.shape[-1]
    count = live[0]
    groups = (count + GROUP - 1) // GROUP

    def load(group):
        slots = pl.ds(group * GROUP, GROUP)
        return pltpu.make_async_copy(tiles.at[slots], buffer.at[slots], sems.at[group])

    def begin(group, carry):
        load(group).start()
        return carry

    lax.fori_loop(0, groups, begin, 0)
    at = 0
    for rows, piece in zip(pieces, sources):
        held[at : at + rows, :] = piece[:rows, :]
        at += rows
    total[...] = jnp.zeros_like(total)
    contract = (((0 if transposed else 1,), (0,)), ((), ()))

    def step(group, carry):
        load(group).wait()
        products = []
        for unit in range(GROUP):
            slot = group * GROUP + unit
            rows = pl.ds(pl.multiple_of(src[slot] * tile, tile), tile)
            values = buffer[slot]
            values = jnp.where(slot < count, values, jnp.zeros_like(values))
            products.append(
                lax.dot_general(values, held[rows, :], contract, preferred_element_type=jnp.float32)
            )
        for unit in range(GROUP):
            rows = pl.ds(pl.multiple_of(dst[group * GROUP + unit] * tile, tile), tile)
            total[rows, :] += products[unit]
        return carry

    lax.fori_loop(0, groups, step, 0)
    at = 0
    for out in outs:
        out[...] = total[at : at + out.shape[0], :].astype(out.dtype)
        at += out.shape[0]


def spmm(transposed, live, dst, src, sources, pieces, tiles, parts):
    slots, tile, _ = tiles.shape
    width = sources[0].shape[1]
    depth = sum(pieces)
    return pl.pallas_call(
        functools.partial(spmm_kernel, transposed, pieces),
        out_shape=[shape(jnp.bfloat16, rows, width) for rows in parts],
        in_specs=[SMEM] * 3 + [VMEM] * len(sources) + [HBM],
        out_specs=[VMEM] * len(parts),
        scratch_shapes=[
            pltpu.VMEM((depth, width), jnp.bfloat16),
            pltpu.VMEM((depth, width), jnp.float32),
            pltpu.VMEM(tiles.shape, tiles.dtype),
            DMA((slots // GROUP,)),
        ],
        compiler_params=params(20),
        cost_estimate=pl.CostEstimate(
            flops=20 * slots * tile * tile * width, bytes_accessed=36 * 2**20, transcendentals=0
        ),
        name="spmm_back" if transposed else "spmm",
    )(live, dst, src, *sources, pltpu.with_memory_space_constraint(tiles, pltpu.HBM))


def add_kernel(first, second, out):
    out[...] = (f32(first) + f32(second)).astype(out.dtype)


def add(first, second):
    return pl.pallas_call(
        add_kernel,
        out_shape=shape(first.dtype, *first.shape),
        in_specs=[VMEM] * 2,
        out_specs=VMEM,
        compiler_params=params(6),
        name="add",
    )(first, second)


def ring_add_kernel(upper, rising, lower, falling, rising_out, falling_out):
    end = rising.shape[0]
    rising_out[:end, :] = (upper[:end, :].astype(jnp.float32) + f32(rising)).astype(upper.dtype)
    if end < upper.shape[0]:
        rising_out[end:, :] = upper[end:, :]
    start = lower.shape[0] - falling.shape[0]
    falling_out[start:, :] = (lower[start:, :].astype(jnp.float32) + f32(falling)).astype(
        lower.dtype
    )
    if start > 0:
        falling_out[:start, :] = lower[:start, :]


def ring_add(upper, rising, lower, falling):
    return pl.pallas_call(
        ring_add_kernel,
        out_shape=[shape(upper.dtype, *upper.shape)] * 2,
        in_specs=[VMEM] * 4,
        out_specs=[VMEM] * 2,
        compiler_params=params(8),
        name="ring_add",
    )(upper, rising, lower, falling)


def part_sum(parts):
    sums = parts[0].astype(jnp.float32)
    for part in range(1, parts.shape[0]):
        sums += parts[part].astype(jnp.float32)
    return sums


def fold_kernel(own, first, second, out):
    out[...] = (f32(own) + f32(first) + f32(second)).astype(out.dtype)


def fold(own, first, second):
    return pl.pallas_call(
        fold_kernel,
        out_shape=shape(own.dtype, *own.shape),
        in_specs=[VMEM] * 3,
        out_specs=VMEM,
        compiler_params=params(4),
        name="fold",
    )(own, first, second)


def whole_sum_kernel(parts, out):
    out[...] = part_sum(parts).astype(out.dtype)


def whole_sum(parts):
    return pl.pallas_call(
        whole_sum_kernel,
        out_shape=shape(parts.dtype, *parts.shape[1:]),
        in_specs=[VMEM],
        out_specs=VMEM,
        compiler_params=params(6),
        name="whole_sum",
    )(parts)


def dense_kernel(chain, last, place, own, other, weight, cotangent, other_cotangent, *refs):
    rows = own.shape[0] // 2
    at_rows = slice(chain * rows, (chain + 1) * rows)
    if last:
        before, terms_before, activated, pair, rising, sums = refs
        activated[: chain * rows, :] = before[...]
    else:
        activated, pair, terms_out = refs
    terms = []
    for at, cot in ((0, cotangent), (rows, other_cotangent)):
        there = rows - at
        aggregated = (
            own[at : at + rows, :].astype(jnp.float32)
            + other[there : there + rows, :].astype(jnp.float32)
        ).astype(jnp.bfloat16)
        pre = jnp.dot(aggregated, weight[...], preferred_element_type=jnp.float32)
        gate = jax.nn.sigmoid(pre)
        slope = gate * (1.0 + pre * (1.0 - gate))
        upstream = (cot[at_rows, :].astype(jnp.float32) * slope).astype(jnp.bfloat16)
        down = lax.dot_general(
            upstream, weight[...], (((1,), (1,)), ((), ())), preferred_element_type=jnp.float32
        ).astype(jnp.bfloat16)
        pair[at : at + rows, :] = down
        if last:
            rising[at : at + rows, :] = down
        terms.append(
            lax.dot_general(
                aggregated, upstream, (((0,), (0,)), ((), ())), preferred_element_type=jnp.float32
            )
        )
        if at == 0:
            activated[at_rows if last else slice(None), :] = (pre * gate).astype(jnp.bfloat16)
    total = terms[0] + terms[1]
    if last:
        along = sums.shape[0]
        sums[...] = (terms_before[...] + total).reshape(sums.shape)
        far = lax.rem(place[0] + along // 2, along)
        rising[2 * rows :, :] = sums[far].astype(rising.dtype)
    else:
        terms_out[...] = total


def dense(chain, place, own, other, weight, cotangent, other_cotangent, along, before=()):
    rows, width = own.shape[0] // 2, own.shape[1]
    part = width // along
    if before:
        out = [
            shape(jnp.bfloat16, (chain + 1) * rows, width),
            shape(jnp.bfloat16, 2 * rows, width),
            shape(jnp.bfloat16, 2 * rows + part, width),
            shape(jnp.float32, along, part, width),
        ]
    else:
        out = [
            shape(jnp.bfloat16, rows, width),
            shape(jnp.bfloat16, 2 * rows, width),
            shape(jnp.float32, width, width),
        ]
    return pl.pallas_call(
        functools.partial(dense_kernel, chain, bool(before)),
        out_shape=out,
        in_specs=[SMEM] + [VMEM] * (5 + len(before)),
        out_specs=[VMEM] * len(out),
        compiler_params=params(16),
        name="dense",
    )(place, own, other, weight, cotangent, other_cotangent, *before)


def pass_on_kernel(cut, offsets, held, place, rising, falling, sums, rising_out, falling_out):
    along, part = sums.shape[:2]
    for first, last, offset, arrived, out in (
        (0, held - cut, offsets[0], rising, rising_out),
        (cut, held, offsets[1], falling, falling_out),
    ):
        out[: last - first, :] = arrived[first:last, :]
        term = sums[lax.rem(place[0] + offset, along)]
        if arrived.shape[0] > held:
            term += arrived[held:, :].astype(jnp.float32)
        out[last - first :, :] = term.astype(out.dtype)


def pass_on(cut, offsets, held, place, rising, falling, sums):
    _, part, width = sums.shape
    return pl.pallas_call(
        functools.partial(pass_on_kernel, cut, offsets, held),
        out_shape=[shape(rising.dtype, held - cut + part, width)] * 2,
        in_specs=[SMEM] + [VMEM] * 3,
        out_specs=[VMEM] * 2,
        compiler_params=params(8),
        name="pass_on",
    )(place, rising, falling, sums)


def relay_kernel(cut, rising, falling, rising_out, falling_out):
    rising_out[...] = rising[: rising_out.shape[0], :]
    falling_out[...] = falling[cut:, :]


def relay(cut, rising, falling):
    rows, width = rising.shape
    return pl.pallas_call(
        functools.partial(relay_kernel, cut),
        out_shape=[shape(rising.dtype, rows - cut, width)] * 2,
        in_specs=[VMEM] * 2,
        out_specs=[VMEM] * 2,
        compiler_params=params(4),
        name="relay",
    )(rising, falling)


def ring_sum_kernel(place, rising, falling, sums, out, stage, sems):
    part = sums.shape[1]
    total = sums[place[0]]
    total += rising[rising.shape[0] - part :, :].astype(jnp.float32)
    total += falling[falling.shape[0] - part :, :].astype(jnp.float32)
    stage[...] = total.astype(stage.dtype)
    copy_all([(stage, out.at[i]) for i in range(out.shape[0])], sems)


def ring_sum(place, rising, falling, sums, copies):
    _, part, width = sums.shape
    return pl.pallas_call(
        ring_sum_kernel,
        out_shape=shape(rising.dtype, copies, part, width),
        in_specs=[SMEM] + [VMEM] * 3,
        out_specs=HBM,
        scratch_shapes=[pltpu.VMEM((part, width), rising.dtype), DMA((copies,))],
        compiler_params=params(4),
        name="ring_sum",
    )(place, rising, falling, sums)


def scaled_sum_kernel(scale, parts, out):
    out[...] = part_sum(parts) * scale


def scaled_sum(parts, scale):
    return pl.pallas_call(
        functools.partial(scaled_sum_kernel, scale),
        out_shape=shape(jnp.float32, *parts.shape[1:]),
        in_specs=[VMEM],
        out_specs=VMEM,
        compiler_params=params(4),
        name="scaled_sum",
    )(parts)


def arrange_kernel(place, *refs):
    pieces, out = refs[:-1], refs[-1]
    part = pieces[0].shape[0]
    for turn, piece in enumerate(pieces):
        at = lax.rem(place[0] + turn, len(pieces))
        out[pl.ds(pl.multiple_of(at * part, part), part), :] = piece[...]


def arrange(place, pieces):
    part, width = pieces[0].shape
    return pl.pallas_call(
        arrange_kernel,
        out_shape=shape(pieces[0].dtype, part * len(pieces), width),
        in_specs=[SMEM] + [VMEM] * len(pieces),
        out_specs=VMEM,
        compiler_params=params(4),
        name="arrange",
    )(place, *pieces)


def body(features, tile_values, tile_rows, tile_cols, tile_counts, weight, cotangent):
    node_rows, width = features.shape[1:]
    slots, tile = tile_values.shape[2:4]
    rows_n, cols_n = lax.axis_size("row"), lax.axis_size("col")
    chips, along = rows_n // 2, cols_n // 2
    core, side = lax.axis_index("row") % 2, lax.axis_index("col") // along
    place = lax.axis_index("col") % along
    same_core = [[2 * k + c for k in range(chips)] for c in range(2)]
    core_swap = [(i, i ^ 1) for i in range(rows_n)]
    side_swap = [(i, (i + along) % cols_n) for i in range(cols_n)]
    up = [(i, i - i % along + (i + 1) % along) for i in range(cols_n)]
    back = [(j, i) for i, j in up]
    live = tile_counts.reshape(1)
    tiles = tile_values.reshape(slots, tile, tile)
    per = node_rows // tile

    col_owner, col_inner = tile_cols.reshape(slots) // per, tile_cols.reshape(slots) % per
    by_core = ((((col_owner % 2) ^ core) * chips) + col_owner // 2) * per + col_inner
    row_owner, row_inner = tile_rows.reshape(slots) // per, tile_rows.reshape(slots) % per
    far = along // 2
    distance = (row_owner % along - place + along) % along
    nearest = jnp.where(
        distance < far, 2 * distance, jnp.where(distance == far, along - 1, 2 * (along - distance) - 1)
    )
    farthest = jnp.where(
        distance == 0, along - 1,
        jnp.where(distance <= far, along - 1 - 2 * distance + (distance == far), 2 * distance - along),
    )
    row_side = (row_owner // along) ^ side
    by_nearest = (row_inner * along + nearest) * 2 + row_side
    by_farthest = (row_inner * along + farthest) * 2 + row_side

    def exchange(x, axis, groups=None):
        return lax.all_to_all(x, axis, 0, 0, axis_index_groups=groups, tiled=True)

    def flat(x):
        return x.reshape(-1, x.shape[-1])

    own = flat(
        exchange(jnp.broadcast_to(features, (chips, node_rows, width)), "row", same_core)
    )
    other = lax.ppermute(own, "row", core_swap)
    pair = 2 * tile
    sizes = [tile] * 2 + [pair] * (along - 1)
    blocks = spmm(
        False, live, by_farthest, by_core, [own, other], [chips * node_rows] * 2, tiles, sizes * per
    )
    chains = range(per)
    blocks = [blocks[c * len(sizes) : (c + 1) * len(sizes)] for c in chains]
    cotangent = cotangent.reshape(node_rows, width)
    other_cotangent = lax.ppermute(cotangent, "col", side_swap)
    rings = [(blocks[c][0], blocks[c][1]) for c in chains]

    def turn(ring):
        return lax.ppermute(ring[0], "col", up), lax.ppermute(ring[1], "col", back)

    for step in range(1, far):
        for c in chains:
            rising, falling = turn(rings[c])
            if step == 1 and c == 0:
                rising, falling, other_cotangent = lax.optimization_barrier(
                    (rising, falling, other_cotangent)
                )
            rings[c] = ring_add(blocks[c][2 * step], rising, blocks[c][2 * step + 1], falling)
    own_sums = [fold(blocks[c][-1], *turn(rings[c])) for c in chains]
    other_sums = [lax.ppermute(own_sums[c], "col", side_swap) for c in chains]
    spot = place.reshape(1)
    dense_args = (weight, cotangent, other_cotangent, along)
    activated, both, terms = dense(0, spot, own_sums[0], other_sums[0], *dense_args)
    activated, both_last, rising, sums = dense(
        1, spot, own_sums[1], other_sums[1], *dense_args, (activated, terms)
    )

    rings = [relay(0, both, both), (rising, both_last)]
    sources = [[both], [both_last]]
    for step in range(1, far + 1):
        for c in chains:
            rings[c] = turn(rings[c])
            sources[c] += rings[c]
            cut = tile if step == far - 1 else 0
            if step == far:
                continue
            if c == per - 1:
                rings[c] = pass_on(
                    cut, (far - step, far + step), pair, spot, *rings[c], sums
                )
            else:
                rings[c] = relay(cut, *rings[c])
    rising, falling = rings[-1]
    sources = sources[0] + sources[1]
    terms = ring_sum(spot, rising, falling, sums, chips)
    terms, *sources = lax.optimization_barrier((terms, *sources))
    terms = exchange(terms, "row", same_core)

    mine, theirs = spmm(
        True, live, by_core, by_nearest, sources, ([pair] * (along - 1) + [tile] * 2) * per,
        tiles, [chips * node_rows] * 2,
    )
    share = scaled_sum(terms, float(node_rows * rows_n * cols_n) ** (-0.5))
    share, mine, theirs = lax.optimization_barrier((share, mine, theirs))
    shares = add(mine, lax.ppermute(theirs, "row", core_swap))
    share = add(share, lax.ppermute(share, "row", core_swap))
    shares = exchange(shares.reshape(chips, node_rows, width), "row", same_core)
    feature_grad = whole_sum(shares)

    turned = [
        lax.ppermute(
            share, "col", [(i, i - i % along + (i - turn) % along) for i in range(cols_n)]
        )
        for turn in range(1, along)
    ]
    weight_grad = arrange(spot, [share] + turned)
    return (
        activated.reshape(1, node_rows, width),
        weight_grad,
        feature_grad.reshape(1, node_rows, width),
    )


def solution(mesh):
    in_specs = (
        P("col", "row", None),
        P("row", "col", None, None, None),
        P("row", "col", None),
        P("row", "col", None),
        P("row", "col"),
        P(),
        P("row", "col", None),
    )
    out_specs = (P("row", "col", None), P(), P("col", "row", None))
    return jax.shard_map(body, mesh=mesh, in_specs=in_specs, out_specs=out_specs, check_vma=False)
```
